32 devices in a mesh: col: 16 (over z, y, x), row: 2 (over core).
Axes of the slice: x: 2, y: 2, z: 4, core: 2. Of those that a mesh axis runs over, the one named last changes fastest.
Arguments:
- slab_embed: float32 [64, 1024], P(None, 'row'), may hold values from -6 to 6
- slab_probe: float32 [32, 1024], P(None, 'row'), may hold values from -6 to 6
- point_embed: float32 [64, 32768], P(None, 'col'), may hold values from -6 to 6
- point_probe: float32 [32, 32768], P(None, 'col'), may hold values from -1.2 to 1.2
- inv_scale: float32 [64], replicated, may hold values from 0.08 to 0.3
Outputs:
- slab_grad: float32 [64, 1024], P(None, 'row')
- point_grad: float32 [64, 32768], P(None, 'col')
The draws below stay inside these ranges and needn't reach their ends.
All inputs are finite; a program needn't handle non-finite values.
Results may differ from the reference program's by a relative error of at most 0.0001.
Values sent between devices are 32-bit elements; how exact they have to be, the bound alone decides.
No kernel may reach another device: no remote copies, remote signals or barrier semaphores. Data moves between devices by JAX's collectives and lax.ppermute only.
A program may use at most 64 MiB of HBM per device.

```python
import math
import jax
import jax.numpy as jnp
from jax import lax

EMB = 64
PROBES = 32
SLAB = 1024
NPTS = 32768


def levels(rng, extent, cuts, low, high):
    def one(axis_at, parts):
        heights = jax.random.uniform(jax.random.fold_in(jax.random.fold_in(rng, 6), axis_at), (parts,), jnp.float32, low / len(cuts), high / len(cuts))
        return jnp.repeat(jnp.exp(heights), extent[axis_at] // parts).reshape((-1,) + (1,) * (len(extent) - axis_at - 1))

    level = one(*cuts[0])
    for cut in cuts[1:]:
        level = level * one(*cut)
    return level


def centred(own_key, extent, deviation, limit, shards=(), held_as=jnp.bfloat16):
    drawn = deviation * jax.random.normal(own_key, extent, jnp.float32)
    if shards:
        drawn = drawn * levels(own_key, extent, shards, -0.22, 0.18)
    return jnp.clip(drawn, -limit, limit).astype(held_as)


def setup_inputs(seed: int = 0) -> dict:
    splits = jax.random.split(jax.random.key(seed), 6)
    slab_embed = centred(splits[0], (EMB, SLAB), 1.0, 6.0, ((1, 2),), jnp.float32)
    slab_probe = centred(splits[1], (PROBES, SLAB), 1.0, 6.0, ((1, 2),), jnp.float32)
    point_embed = centred(splits[2], (EMB, NPTS), 1.0, 6.0, ((1, 16),), jnp.float32)
    point_probe = centred(splits[3], (PROBES, NPTS), 0.2, 1.2, ((1, 16),), jnp.float32)
    inv_scale = jnp.clip(jnp.exp(jax.random.uniform(splits[4], (EMB,), jnp.float32, math.log(0.08), math.log(0.3))), 0.08, 0.3)
    return dict(slab_embed=slab_embed, slab_probe=slab_probe, point_embed=point_embed, point_probe=point_probe, inv_scale=inv_scale)


def reference(slab_embed, slab_probe, point_embed, point_probe, inv_scale):
    hp = lax.Precision.HIGHEST
    weight_sq = inv_scale * inv_scale
    scaled = slab_embed * weight_sq[:, None]
    self_term = jnp.sum(scaled * slab_embed, axis=0)
    width = min(4096, NPTS)
    count = NPTS // width
    embed_blocks = point_embed.reshape(EMB, count, width).transpose(1, 0, 2)
    probe_blocks = point_probe.reshape(PROBES, count, width).transpose(1, 0, 2)

    def step(carry, item):
        row_total, mixed = carry
        points, probes = item
        other_term = jnp.sum(weight_sq[:, None] * points * points, axis=0)
        cross = jnp.dot(scaled.T, points, precision=hp)
        kernel = jnp.exp(-0.5 * (self_term[:, None] + other_term[None, :] - 2.0 * cross))
        weights = kernel * jnp.dot(slab_probe.T, probes, precision=hp)
        row_total = row_total + jnp.sum(weights, axis=1)
        mixed = mixed + jnp.dot(points, weights.T, precision=hp)
        grad_block = weight_sq[:, None] * (jnp.dot(slab_embed, weights, precision=hp) - points * jnp.sum(weights, axis=0)[None, :])
        return (row_total, mixed), grad_block

    start = (jnp.zeros((SLAB,), jnp.float32), jnp.zeros((EMB, SLAB), jnp.float32))
    (row_total, mixed), grads = lax.scan(step, start, (embed_blocks, probe_blocks))
    slab_grad = -weight_sq[:, None] * (slab_embed * row_total[None, :] - mixed)
    point_grad = grads.transpose(1, 0, 2).reshape(EMB, NPTS)
    return slab_grad, point_grad
```

```python
import functools

import jax
import jax.numpy as jnp
from jax import lax
from jax.experimental import pallas as pl
from jax.experimental.pallas import tpu as pltpu
from jax.sharding import PartitionSpec as P

f32, bf16 = jnp.float32, jnp.bfloat16
VMEM_LIMIT = 40 * 2**20


def split(value, parts):
    terms = []
    for _ in range(parts - 1):
        terms.append(value.astype(bf16))
        value = value - terms[-1].astype(f32)
    return terms + [value.astype(bf16)]


def stacked_rows(values, width):
    at = lax.broadcasted_iota(jnp.int32, (16, width), 0)
    block = jnp.zeros((16, width), f32)
    for place, value in enumerate(values):
        block = jnp.where(at == place, value, block)
    return block.astype(bf16)


def pad_rows(blocks, width):
    depth = sum(block.shape[0] for block in blocks)
    short = -depth % 256
    return jnp.concatenate(blocks + ([jnp.zeros((short, width), bf16)] if short else []), axis=0)


def column_weight(inv_ref, emb):
    inv = inv_ref[...]
    return jnp.broadcast_to(inv * inv, (128, emb)).T[:, :1]


def dot(x, y):
    return jnp.dot(x, y, preferred_element_type=f32)


def slab_kernel(width, slab_hbm, slab_probe_hbm, points_hbm, probes_hbm, inv_hbm, terms_ref, high_ref, low_ref,
                slab_ref, slab_probe_ref, points_ref, probes_ref, inv_ref, left, left_probe, total, sems):
    emb, rows = slab_ref.shape
    count = points_ref.shape[1] // width
    pairs = ((inv_hbm, inv_ref), (slab_hbm, slab_ref), (slab_probe_hbm, slab_probe_ref),
             (points_hbm, points_ref), (probes_hbm, probes_ref))
    copies = [pltpu.make_async_copy(src, dst, sems.at[k]) for k, (src, dst) in enumerate(pairs)]
    for copy in copies:
        copy.start()
    for copy in copies[:3]:
        copy.wait()
    weight = column_weight(inv_ref, emb)
    slab = slab_ref[...]
    scaled = slab * weight
    one = jnp.ones((1, rows), f32)
    self_terms = [v.astype(f32) for v in split(-0.5 * jnp.sum(scaled * slab, axis=0, keepdims=True), 3)]
    s1, s2, s3 = split(scaled, 3)
    left[...] = pad_rows([s1, s1, s2, s1, s2, s3, stacked_rows([one] * 3 + self_terms, rows)], rows).T
    p1, p2, p3 = split(slab_probe_ref[...], 3)
    left_probe[...] = pad_rows([p1, p1, p2, p1, p2, p3], rows).T
    for copy in copies[3:]:
        copy.wait()
    one = jnp.ones((1, width), f32)
    for block in range(count):
        columns = pl.ds(block * width, width)
        points = points_ref[:, columns]
        other_terms = [v.astype(f32) for v in split(-0.5 * jnp.sum(weight * points * points, axis=0, keepdims=True), 3)]
        x1, x2, x3 = split(points, 3)
        right = pad_rows([x1, x2, x1, x3, x2, x1, stacked_rows(other_terms + [one] * 3, width)], width)
        q1, q2, q3 = split(probes_ref[:, columns], 3)
        right_probe = pad_rows([q1, q2, q1, q3, q2, q1], width)
        weights = jnp.exp(dot(left[...], right)) * dot(left_probe[...], right_probe)
        high, low = split(weights, 2)
        high_ref[:, columns] = high
        low_ref[:, columns] = low
        both = jnp.concatenate([x1, x2, stacked_rows([one], width)], axis=0)
        nt = (((1,), (1,)), ((), ()))
        part = lax.dot_general(high, both, nt, preferred_element_type=f32) + lax.dot_general(
            low, both, nt, preferred_element_type=f32
        )
        total[...] = part if block == 0 else total[...] + part
    mixed = total[:, : 2 * emb].T
    row_total = total[:, 2 * emb :].T
    terms_ref[...] = -weight * (slab * row_total[:1] - (mixed[:emb] + mixed[emb:]))


def slab_call(slab, slab_probe, points, probes, inv, width):
    emb, rows = slab.shape
    count = points.shape[1]
    any_space = pl.BlockSpec(memory_space=pl.ANY)
    vmem = pl.BlockSpec(memory_space=pltpu.VMEM)
    shapes = [slab.shape, slab_probe.shape, points.shape, probes.shape, inv.shape]
    return pl.pallas_call(
        functools.partial(slab_kernel, width),
        out_shape=(
            jax.ShapeDtypeStruct((emb, rows), f32),
            jax.ShapeDtypeStruct((rows, count), bf16),
            jax.ShapeDtypeStruct((rows, count), bf16),
        ),
        in_specs=[any_space] * 5,
        out_specs=[vmem] * 3,
        scratch_shapes=[pltpu.VMEM(shape, f32) for shape in shapes]
        + [
            pltpu.VMEM((rows, 512), bf16),
            pltpu.VMEM((rows, 256), bf16),
            pltpu.VMEM((rows, 2 * emb + 16), f32),
            pltpu.SemaphoreType.DMA((5,)),
        ],
        compiler_params=pltpu.CompilerParams(vmem_limit_bytes=VMEM_LIMIT),
        cost_estimate=pl.CostEstimate(flops=9 * 10**9, bytes_accessed=5 * 10**6, transcendentals=rows * count),
        name="slab_terms",
    )(slab, slab_probe, points, probes, inv)


def point_kernel(width, slab_ref, points_ref, inv_ref, high_ref, low_ref, terms_ref):
    emb, rows = slab_ref.shape
    weight = column_weight(inv_ref, emb)
    s1, s2 = split(slab_ref[...], 2)
    left = jnp.concatenate([s1, s2, stacked_rows([jnp.ones((1, rows), f32)], rows)], axis=0)
    for block in range(points_ref.shape[1] // width):
        columns = pl.ds(block * width, width)
        sums = dot(left, high_ref[:, columns]) + dot(left, low_ref[:, columns])
        terms_ref[:, columns] = weight * (
            sums[:emb] + sums[emb : 2 * emb] - points_ref[:, columns] * sums[2 * emb : 2 * emb + 1]
        )


def point_call(slab, points, inv, high, low, width):
    rows, count = high.shape
    vmem = pl.BlockSpec(memory_space=pltpu.VMEM)
    return pl.pallas_call(
        functools.partial(point_kernel, width),
        out_shape=jax.ShapeDtypeStruct(points.shape, f32),
        in_specs=[vmem] * 5,
        out_specs=vmem,
        compiler_params=pltpu.CompilerParams(vmem_limit_bytes=VMEM_LIMIT),
        cost_estimate=pl.CostEstimate(flops=2 * 10**9, bytes_accessed=5 * 10**6, transcendentals=0),
        name="point_terms",
    )(slab, points, inv, high, low)


def sum_over(value, axis, size):
    if size & (size - 1):
        return lax.psum(value, axis)
    step = 1
    while step < size:
        value = value + lax.ppermute(value, axis, [(k, k ^ step) for k in range(size)])
        step *= 2
    return value


def solution(mesh):
    def local(slab_embed, slab_probe, point_embed, point_probe, inv_scale):
        inv = inv_scale.reshape(1, -1)
        width = 512 if point_embed.shape[1] % 512 == 0 else point_embed.shape[1]
        slab_terms, high, low = slab_call(slab_embed, slab_probe, point_embed, point_probe, inv, width)
        point_terms = point_call(slab_embed, point_embed, inv, high, low, width)
        slab_grad = sum_over(slab_terms, "col", mesh.shape["col"])
        point_grad = sum_over(point_terms, "row", mesh.shape["row"])
        return slab_grad, point_grad

    placed = (P(None, "row"), P(None, "row"), P(None, "col"), P(None, "col"), P())
    return jax.shard_map(
        local, mesh=mesh, in_specs=placed, out_specs=(P(None, "row"), P(None, "col")), check_vma=False
    )
```

```python
import functools

import jax
import jax.numpy as jnp
from jax import lax
from jax.experimental import pallas as pl
from jax.experimental.pallas import tpu as pltpu
from jax.sharding import PartitionSpec as P

f32, bf16 = jnp.float32, jnp.bfloat16
VMEM_LIMIT = 40 * 2**20


def split(value, parts):
    terms = []
    for _ in range(parts - 1):
        terms.append(value.astype(bf16))
        value = value - terms[-1].astype(f32)
    return terms + [value.astype(bf16)]


def stacked_rows(values, width):
    at = lax.broadcasted_iota(jnp.int32, (16, width), 0)
    block = jnp.zeros((16, width), f32)
    for place, value in enumerate(values):
        block = jnp.where(at == place, value, block)
    return block.astype(bf16)


def pad_rows(blocks, width):
    depth = sum(block.shape[0] for block in blocks)
    short = -depth % 256
    return jnp.concatenate(blocks + ([jnp.zeros((short, width), bf16)] if short else []), axis=0)


def column_weight(inv_ref, emb):
    inv = inv_ref[...]
    return jnp.broadcast_to(inv * inv, (128, emb)).T[:, :1]


def dot(x, y):
    return jnp.dot(x, y, preferred_element_type=f32)


def slab_kernel(width, slab_hbm, slab_probe_hbm, points_hbm, probes_hbm, inv_hbm, terms_ref, high_ref, low_ref,
                slab_ref, slab_probe_ref, points_ref, probes_ref, inv_ref, left, left_probe, total, sems):
    emb, rows = slab_ref.shape
    columns = [pl.ds(block * width, width) for block in range(points_ref.shape[1] // width)]
    pairs = [(inv_hbm, inv_ref), (slab_hbm, slab_ref), (slab_probe_hbm, slab_probe_ref)]
    for here in columns:
        pairs += [(points_hbm.at[:, here], points_ref.at[:, here]), (probes_hbm.at[:, here], probes_ref.at[:, here])]
    arriving = [pltpu.make_async_copy(src, dst, sems.at[k]) for k, (src, dst) in enumerate(pairs)]
    for copy in arriving:
        copy.start()
    for copy in arriving[:3]:
        copy.wait()
    weight = column_weight(inv_ref, emb)
    slab = slab_ref[...]
    scaled = slab * weight
    one = jnp.ones((1, rows), f32)
    self_terms = [v.astype(f32) for v in split(-0.5 * jnp.sum(scaled * slab, axis=0, keepdims=True), 3)]
    s1, s2, s3 = split(scaled, 3)
    left[...] = pad_rows([s1, s1, s2, s1, s2, s3, stacked_rows([one] * 3 + self_terms, rows)], rows).T
    p1, p2, p3 = split(slab_probe_ref[...], 3)
    left_probe[...] = pad_rows([p1, p1, p2, p1, p2, p3], rows).T
    one = jnp.ones((1, width), f32)
    for block, here in enumerate(columns):
        for copy in arriving[3 + 2 * block : 5 + 2 * block]:
            copy.wait()
        points = points_ref[:, here]
        other_terms = [v.astype(f32) for v in split(-0.5 * jnp.sum(weight * points * points, axis=0, keepdims=True), 3)]
        x1, x2, x3 = split(points, 3)
        right = pad_rows([x1, x2, x1, x3, x2, x1, stacked_rows(other_terms + [one] * 3, width)], width)
        q1, q2, q3 = split(probes_ref[:, here], 3)
        right_probe = pad_rows([q1, q2, q1, q3, q2, q1], width)
        weights = jnp.exp(dot(left[...], right)) * dot(left_probe[...], right_probe)
        high, low = split(weights, 2)
        high_ref[:, here] = high
        low_ref[:, here] = low
        both = jnp.concatenate([x1, x2, stacked_rows([one], width)], axis=0)
        nt = (((1,), (1,)), ((), ()))
        part = lax.dot_general(high, both, nt, preferred_element_type=f32) + lax.dot_general(
            low, both, nt, preferred_element_type=f32
        )
        total[...] = part if block == 0 else total[...] + part
    mixed = total[:, : 2 * emb].T
    row_total = total[:, 2 * emb :].T
    terms_ref[...] = -weight * (slab * row_total[:1] - (mixed[:emb] + mixed[emb:]))


def slab_call(slab, slab_probe, points, probes, inv, width):
    emb, rows = slab.shape
    count = points.shape[1]
    operands = [pltpu.with_memory_space_constraint(v, pltpu.HBM) for v in (slab, slab_probe, points, probes, inv)]
    return pl.pallas_call(
        functools.partial(slab_kernel, width),
        out_shape=(pltpu.VMEM((emb, rows), f32), pltpu.VMEM((rows, count), bf16), pltpu.VMEM((rows, count), bf16)),
        in_specs=[pl.BlockSpec(memory_space=pltpu.HBM)] * 5,
        out_specs=[pl.BlockSpec(memory_space=pltpu.VMEM)] * 3,
        scratch_shapes=[pltpu.VMEM(v.shape, f32) for v in operands]
        + [
            pltpu.VMEM((rows, 512), bf16),
            pltpu.VMEM((rows, 256), bf16),
            pltpu.VMEM((rows, 2 * emb + 16), f32),
            pltpu.SemaphoreType.DMA((3 + 2 * (count // width),)),
        ],
        compiler_params=pltpu.CompilerParams(vmem_limit_bytes=VMEM_LIMIT),
        cost_estimate=pl.CostEstimate(flops=9 * 10**9, bytes_accessed=5 * 10**6, transcendentals=rows * count),
        name="slab_terms",
    )(*operands)


def point_kernel(width, slab_ref, points_ref, inv_ref, high_ref, low_ref, terms_ref):
    emb, rows = slab_ref.shape
    weight = column_weight(inv_ref, emb)
    s1, s2 = split(slab_ref[...], 2)
    left = jnp.concatenate([s1, s2, stacked_rows([jnp.ones((1, rows), f32)], rows)], axis=0)
    for block in range(points_ref.shape[1] // width):
        columns = pl.ds(block * width, width)
        sums = dot(left, high_ref[:, columns]) + dot(left, low_ref[:, columns])
        terms_ref[:, columns] = weight * (
            sums[:emb] + sums[emb : 2 * emb] - points_ref[:, columns] * sums[2 * emb : 2 * emb + 1]
        )


def point_call(slab, points, inv, high, low, width):
    rows, count = high.shape
    vmem = pl.BlockSpec(memory_space=pltpu.VMEM)
    return pl.pallas_call(
        functools.partial(point_kernel, width),
        out_shape=jax.ShapeDtypeStruct(points.shape, f32),
        in_specs=[vmem] * 5,
        out_specs=vmem,
        compiler_params=pltpu.CompilerParams(vmem_limit_bytes=VMEM_LIMIT),
        cost_estimate=pl.CostEstimate(flops=2 * 10**9, bytes_accessed=5 * 10**6, transcendentals=0),
        name="point_terms",
    )(slab, points, inv, high, low)


def sum_over(value, axis, size, beside=None):
    if size & (size - 1):
        return lax.psum(value, axis), beside
    steps = [1 << bit for bit in range(size.bit_length() - 1)]
    for place, step in enumerate(steps):
        other = lax.ppermute(value, axis, [(k, k ^ step) for k in range(size)])
        if place == len(steps) - 1 and beside is not None:
            other, beside = lax.optimization_barrier((other, beside))
        value = value + other
    return value, beside


def solution(mesh):
    def local(slab_embed, slab_probe, point_embed, point_probe, inv_scale):
        inv = inv_scale.reshape(1, -1)
        width = 512 if point_embed.shape[1] % 512 == 0 else point_embed.shape[1]
        slab_terms, high, low = slab_call(slab_embed, slab_probe, point_embed, point_probe, inv, width)
        point_terms = point_call(slab_embed, point_embed, inv, high, low, width)
        point_grad, _ = sum_over(point_terms, "row", mesh.shape["row"])
        slab_grad, point_grad = sum_over(slab_terms, "col", mesh.shape["col"], beside=point_grad)
        return slab_grad, point_grad

    placed = (P(None, "row"), P(None, "row"), P(None, "col"), P(None, "col"), P())
    return jax.shard_map(
        local, mesh=mesh, in_specs=placed, out_specs=(P(None, "row"), P(None, "col")), check_vma=False
    )
```

```python
import functools

import jax
import jax.numpy as jnp
from jax import lax
from jax.experimental import pallas as pl
from jax.experimental.pallas import tpu as pltpu
from jax.sharding import PartitionSpec as P

f32, bf16 = jnp.float32, jnp.bfloat16
VMEM_LIMIT = 40 * 2**20


def split(value, parts):
    terms = []
    for _ in range(parts - 1):
        terms.append(value.astype(bf16))
        value = value - terms[-1].astype(f32)
    return terms + [value.astype(bf16)]


def stacked_rows(values, width):
    at = lax.broadcasted_iota(jnp.int32, (16, width), 0)
    block = jnp.zeros((16, width), f32)
    for place, value in enumerate(values):
        block = jnp.where(at == place, value, block)
    return block.astype(bf16)


def pad_rows(blocks, width):
    depth = sum(block.shape[0] for block in blocks)
    short = -depth % 256
    return jnp.concatenate(blocks + ([jnp.zeros((short, width), bf16)] if short else []), axis=0)


def column_weight(inv_ref, emb):
    inv = inv_ref[...]
    return jnp.broadcast_to(inv * inv, (128, emb)).T[:, :1]


def dot(x, y):
    return jnp.dot(x, y, preferred_element_type=f32)


def slab_kernel(width, slab_hbm, slab_probe_hbm, points_hbm, probes_hbm, inv_hbm, terms_ref, high_ref, low_ref,
                slab_ref, slab_probe_ref, points_ref, probes_ref, inv_ref, left, left_probe, total, sems):
    emb, rows = slab_ref.shape
    columns = [pl.ds(block * width, width) for block in range(points_ref.shape[1] // width)]
    pairs = [(inv_hbm, inv_ref), (slab_hbm, slab_ref), (slab_probe_hbm, slab_probe_ref)]
    pairs += [(points_hbm, points_ref), (probes_hbm, probes_ref)]
    arriving = [pltpu.make_async_copy(src, dst, sems.at[k]) for k, (src, dst) in enumerate(pairs)]
    for copy in arriving:
        copy.start()
    for copy in arriving[:3]:
        copy.wait()
    weight = column_weight(inv_ref, emb)
    slab = slab_ref[...]
    scaled = slab * weight
    one = jnp.ones((1, rows), f32)
    self_terms = [v.astype(f32) for v in split(-0.5 * jnp.sum(scaled * slab, axis=0, keepdims=True), 3)]
    s1, s2, s3 = split(scaled, 3)
    left[...] = pad_rows([s1, s1, s2, s1, s2, s3, stacked_rows([one] * 3 + self_terms, rows)], rows).T
    p1, p2, p3 = split(slab_probe_ref[...], 3)
    left_probe[...] = pad_rows([p1, p1, p2, p1, p2, p3], rows).T
    for copy in arriving[3:]:
        copy.wait()
    one = jnp.ones((1, width), f32)
    for block, here in enumerate(columns):
        points = points_ref[:, here]
        other_terms = [v.astype(f32) for v in split(-0.5 * jnp.sum(weight * points * points, axis=0, keepdims=True), 3)]
        x1, x2, x3 = split(points, 3)
        right = pad_rows([x1, x2, x1, x3, x2, x1, stacked_rows(other_terms + [one] * 3, width)], width)
        q1, q2, q3 = split(probes_ref[:, here], 3)
        right_probe = pad_rows([q1, q2, q1, q3, q2, q1], width)
        weights = jnp.exp(dot(left[...], right)) * dot(left_probe[...], right_probe)
        high, low = split(weights, 2)
        high_ref[:, here] = high
        low_ref[:, here] = low
        both = jnp.concatenate([x1, x2, stacked_rows([one], width)], axis=0)
        nt = (((1,), (1,)), ((), ()))
        part = lax.dot_general(high, both, nt, preferred_element_type=f32) + lax.dot_general(
            low, both, nt, preferred_element_type=f32
        )
        total[...] = part if block == 0 else total[...] + part
    mixed = total[:, : 2 * emb].T
    row_total = total[:, 2 * emb :].T
    terms_ref[...] = -weight * (slab * row_total[:1] - (mixed[:emb] + mixed[emb:]))


def slab_call(slab, slab_probe, points, probes, inv, width):
    emb, rows = slab.shape
    count = points.shape[1]
    operands = [pltpu.with_memory_space_constraint(v, pltpu.HBM) for v in (slab, slab_probe, points, probes, inv)]
    return pl.pallas_call(
        functools.partial(slab_kernel, width),
        out_shape=(pltpu.VMEM((emb, rows), f32), pltpu.VMEM((rows, count), bf16), pltpu.VMEM((rows, count), bf16)),
        in_specs=[pl.BlockSpec(memory_space=pltpu.HBM)] * 5,
        out_specs=[pl.BlockSpec(memory_space=pltpu.VMEM)] * 3,
        scratch_shapes=[pltpu.VMEM(v.shape, f32) for v in operands]
        + [
            pltpu.VMEM((rows, 512), bf16),
            pltpu.VMEM((rows, 256), bf16),
            pltpu.VMEM((rows, 2 * emb + 16), f32),
            pltpu.SemaphoreType.DMA((5,)),
        ],
        compiler_params=pltpu.CompilerParams(vmem_limit_bytes=VMEM_LIMIT),
        cost_estimate=pl.CostEstimate(flops=9 * 10**9, bytes_accessed=5 * 10**6, transcendentals=rows * count),
        name="slab_terms",
    )(*operands)


def point_kernel(width, slab_ref, points_ref, inv_ref, high_ref, low_ref, terms_ref):
    emb, rows = slab_ref.shape
    weight = column_weight(inv_ref, emb)
    s1, s2 = split(slab_ref[...], 2)
    left = jnp.concatenate([s1, s2, stacked_rows([jnp.ones((1, rows), f32)], rows)], axis=0)
    for block in range(points_ref.shape[1] // width):
        columns = pl.ds(block * width, width)
        sums = dot(left, high_ref[:, columns]) + dot(left, low_ref[:, columns])
        terms_ref[:, columns] = weight * (
            sums[:emb] + sums[emb : 2 * emb] - points_ref[:, columns] * sums[2 * emb : 2 * emb + 1]
        )


def point_call(slab, points, inv, high, low, width):
    rows, count = high.shape
    vmem = pl.BlockSpec(memory_space=pltpu.VMEM)
    return pl.pallas_call(
        functools.partial(point_kernel, width),
        out_shape=jax.ShapeDtypeStruct(points.shape, f32),
        in_specs=[vmem] * 5,
        out_specs=vmem,
        compiler_params=pltpu.CompilerParams(vmem_limit_bytes=VMEM_LIMIT),
        cost_estimate=pl.CostEstimate(flops=2 * 10**9, bytes_accessed=5 * 10**6, transcendentals=0),
        name="point_terms",
    )(slab, points, inv, high, low)


def sum_over(value, axis, size, beside=None):
    if size & (size - 1):
        return lax.psum(value, axis), beside
    steps = [1 << bit for bit in range(size.bit_length() - 1)]
    for place, step in enumerate(steps):
        other = lax.ppermute(value, axis, [(k, k ^ step) for k in range(size)])
        if place == len(steps) - 1 and beside is not None:
            other, beside = lax.optimization_barrier((other, beside))
        value = value + other
    return value, beside


def sum_over_columns(value, mesh, beside):
    size, others = mesh.shape["col"], mesh.shape["row"]
    if size & (size - 1):
        return lax.psum(value, "col"), beside
    bits = [1 << bit for bit in range(size.bit_length() - 1)]
    even = [bits.pop(len(bits) // 2)] + bits
    odd = [even[k ^ 1] if k ^ 1 < len(even) else even[k] for k in range(len(even))]
    for place in range(len(even)):
        pairs = [
            (col * others + row, (col ^ (odd if row % 2 else even)[place]) * others + row)
            for col in range(size)
            for row in range(others)
        ]
        other = lax.ppermute(value, ("col", "row"), pairs)
        if place == len(even) - 1:
            other, beside = lax.optimization_barrier((other, beside))
        value = value + other
    return value, beside


def solution(mesh):
    def local(slab_embed, slab_probe, point_embed, point_probe, inv_scale):
        inv = inv_scale.reshape(1, -1)
        width = 512 if point_embed.shape[1] % 512 == 0 else point_embed.shape[1]
        slab_terms, high, low = slab_call(slab_embed, slab_probe, point_embed, point_probe, inv, width)
        point_terms = point_call(slab_embed, point_embed, inv, high, low, width)
        point_grad, _ = sum_over(point_terms, "row", mesh.shape["row"])
        slab_grad, point_grad = sum_over_columns(slab_terms, mesh, point_grad)
        return slab_grad, point_grad

    placed = (P(None, "row"), P(None, "row"), P(None, "col"), P(None, "col"), P())
    return jax.shard_map(
        local, mesh=mesh, in_specs=placed, out_specs=(P(None, "row"), P(None, "col")), check_vma=False
    )
```

```python
import functools

import jax
import jax.numpy as jnp
from jax import lax
from jax.experimental import pallas as pl
from jax.experimental.pallas import tpu as pltpu
from jax.sharding import PartitionSpec as P

f32, bf16 = jnp.float32, jnp.bfloat16
VMEM_LIMIT = 40 * 2**20


def split(value, parts):
    terms = []
    for _ in range(parts - 1):
        terms.append(value.astype(bf16))
        value = value - terms[-1].astype(f32)
    return terms + [value.astype(bf16)]


def stacked_rows(values, width):
    at = lax.broadcasted_iota(jnp.int32, (16, width), 0)
    block = jnp.zeros((16, width), f32)
    for place, value in enumerate(values):
        block = jnp.where(at == place, value, block)
    return block.astype(bf16)


def pad_rows(blocks, width):
    depth = sum(block.shape[0] for block in blocks)
    short = -depth % 256
    return jnp.concatenate(blocks + ([jnp.zeros((short, width), bf16)] if short else []), axis=0)


def column_weight(inv_ref, emb):
    inv = inv_ref[...]
    return jnp.broadcast_to(inv * inv, (128, emb)).T[:, :1]


def dot(x, y):
    return jnp.dot(x, y, preferred_element_type=f32)


def slab_kernel(width, slab_hbm, slab_probe_hbm, points_hbm, probes_hbm, inv_hbm, terms_ref, high_ref, low_ref,
                slab_ref, slab_probe_ref, points_ref, probes_ref, inv_ref, left, left_probe, total, sems):
    emb, rows = slab_ref.shape
    columns = [pl.ds(block * width, width) for block in range(points_ref.shape[1] // width)]
    pairs = [(inv_hbm, inv_ref), (slab_hbm, slab_ref), (slab_probe_hbm, slab_probe_ref)]
    pairs += [(points_hbm, points_ref), (probes_hbm, probes_ref)]
    arriving = [pltpu.make_async_copy(src, dst, sems.at[k]) for k, (src, dst) in enumerate(pairs)]
    for copy in arriving:
        copy.start()
    for copy in arriving[:3]:
        copy.wait()
    weight = column_weight(inv_ref, emb)
    slab = slab_ref[...]
    scaled = slab * weight
    one = jnp.ones((1, rows), f32)
    self_terms = [v.astype(f32) for v in split(-0.5 * jnp.sum(scaled * slab, axis=0, keepdims=True), 3)]
    s1, s2, s3 = split(scaled, 3)
    left[...] = pad_rows([s1, s1, s2, s1, s2, s3, stacked_rows([one] * 3 + self_terms, rows)], rows).T
    p1, p2, p3 = split(slab_probe_ref[...], 3)
    left_probe[...] = pad_rows([p1, p1, p2, p1, p2, p3], rows).T
    for copy in arriving[3:]:
        copy.wait()
    one = jnp.ones((1, width), f32)
    for block, here in enumerate(columns):
        points = points_ref[:, here]
        other_terms = [v.astype(f32) for v in split(-0.5 * jnp.sum(weight * points * points, axis=0, keepdims=True), 3)]
        x1, x2, x3 = split(points, 3)
        right = pad_rows([x1, x2, x1, x3, x2, x1, stacked_rows(other_terms + [one] * 3, width)], width)
        q1, q2, q3 = split(probes_ref[:, here], 3)
        right_probe = pad_rows([q1, q2, q1, q3, q2, q1], width)
        weights = jnp.exp(dot(left[...], right)) * dot(left_probe[...], right_probe)
        high, low = split(weights, 2)
        high_ref[:, here] = high
        low_ref[:, here] = low
        both = jnp.concatenate([x1, x2, x3, stacked_rows([one], width)], axis=0)
        nt = (((1,), (1,)), ((), ()))
        part = lax.dot_general(high, both, nt, preferred_element_type=f32) + lax.dot_general(
            low, both, nt, preferred_element_type=f32
        )
        total[...] = part if block == 0 else total[...] + part
    sums = total[...].T
    mixed = sums[:emb] + (sums[emb : 2 * emb] + sums[2 * emb : 3 * emb])
    terms_ref[...] = -weight * (slab * sums[3 * emb : 3 * emb + 1] - mixed)


def slab_call(slab, slab_probe, points, probes, inv, width):
    emb, rows = slab.shape
    count = points.shape[1]
    operands = [pltpu.with_memory_space_constraint(v, pltpu.HBM) for v in (slab, slab_probe, points, probes, inv)]
    return pl.pallas_call(
        functools.partial(slab_kernel, width),
        out_shape=(pltpu.VMEM((emb, rows), f32), pltpu.VMEM((rows, count), bf16), pltpu.VMEM((rows, count), bf16)),
        in_specs=[pl.BlockSpec(memory_space=pltpu.HBM)] * 5,
        out_specs=[pl.BlockSpec(memory_space=pltpu.VMEM)] * 3,
        scratch_shapes=[pltpu.VMEM(v.shape, f32) for v in operands]
        + [
            pltpu.VMEM((rows, 512), bf16),
            pltpu.VMEM((rows, 256), bf16),
            pltpu.VMEM((rows, 3 * emb + 16), f32),
            pltpu.SemaphoreType.DMA((5,)),
        ],
        compiler_params=pltpu.CompilerParams(vmem_limit_bytes=VMEM_LIMIT),
        cost_estimate=pl.CostEstimate(flops=9 * 10**9, bytes_accessed=5 * 10**6, transcendentals=rows * count),
        name="slab_terms",
    )(*operands)


def point_kernel(width, slab_ref, points_ref, inv_ref, high_ref, low_ref, terms_ref):
    emb, rows = slab_ref.shape
    weight = column_weight(inv_ref, emb)
    s1, s2, s3 = split(slab_ref[...], 3)
    left = jnp.concatenate([s1, s2, s3, stacked_rows([jnp.ones((1, rows), f32)], rows)], axis=0)
    for block in range(points_ref.shape[1] // width):
        columns = pl.ds(block * width, width)
        sums = dot(left, high_ref[:, columns]) + dot(left, low_ref[:, columns])
        mixed = sums[:emb] + (sums[emb : 2 * emb] + sums[2 * emb : 3 * emb])
        terms_ref[:, columns] = weight * (mixed - points_ref[:, columns] * sums[3 * emb : 3 * emb + 1])


def point_call(slab, points, inv, high, low, width):
    rows, count = high.shape
    vmem = pl.BlockSpec(memory_space=pltpu.VMEM)
    return pl.pallas_call(
        functools.partial(point_kernel, width),
        out_shape=jax.ShapeDtypeStruct(points.shape, f32),
        in_specs=[vmem] * 5,
        out_specs=vmem,
        compiler_params=pltpu.CompilerParams(vmem_limit_bytes=VMEM_LIMIT),
        cost_estimate=pl.CostEstimate(flops=2 * 10**9, bytes_accessed=5 * 10**6, transcendentals=0),
        name="point_terms",
    )(slab, points, inv, high, low)


def sum_over(value, axis, size, beside=None):
    if size & (size - 1):
        return lax.psum(value, axis), beside
    steps = [1 << bit for bit in range(size.bit_length() - 1)]
    for place, step in enumerate(steps):
        other = lax.ppermute(value, axis, [(k, k ^ step) for k in range(size)])
        if place == len(steps) - 1 and beside is not None:
            other, beside = lax.optimization_barrier((other, beside))
        value = value + other
    return value, beside


def sum_over_columns(value, mesh, beside):
    size, others = mesh.shape["col"], mesh.shape["row"]
    if size & (size - 1):
        return lax.psum(value, "col"), beside
    bits = [1 << bit for bit in range(size.bit_length() - 1)]
    first = bits.pop(len(bits) // 2)
    even = [first] + bits
    odd = [even[k ^ 1] if k ^ 1 < len(even) else even[k] for k in range(len(even))]
    late = even[:-2] + even[:-3:-1] if len(even) > 3 else even
    for place in range(len(even)):
        pairs = [
            (col * others + row, (col ^ (odd if row % 2 else late if col & first else even)[place]) * others + row)
            for col in range(size)
            for row in range(others)
        ]
        other = lax.ppermute(value, ("col", "row"), pairs)
        if place == len(even) - 1:
            other, beside = lax.optimization_barrier((other, beside))
        value = value + other
    return value, beside


def solution(mesh):
    def local(slab_embed, slab_probe, point_embed, point_probe, inv_scale):
        inv = inv_scale.reshape(1, -1)
        width = 512 if point_embed.shape[1] % 512 == 0 else point_embed.shape[1]
        slab_terms, high, low = slab_call(slab_embed, slab_probe, point_embed, point_probe, inv, width)
        point_terms = point_call(slab_embed, point_embed, inv, high, low, width)
        point_grad, _ = sum_over(point_terms, "row", mesh.shape["row"])
        slab_grad, point_grad = sum_over_columns(slab_terms, mesh, point_grad)
        return slab_grad, point_grad

    placed = (P(None, "row"), P(None, "row"), P(None, "col"), P(None, "col"), P())
    return jax.shard_map(
        local, mesh=mesh, in_specs=placed, out_specs=(P(None, "row"), P(None, "col")), check_vma=False
    )
```

```python
import functools

import jax
import jax.numpy as jnp
from jax import lax
from jax.experimental import pallas as pl
from jax.experimental.pallas import tpu as pltpu
from jax.sharding import PartitionSpec as P

f32, bf16 = jnp.float32, jnp.bfloat16
VMEM_LIMIT = 40 * 2**20


def split(value, parts):
    terms = []
    for _ in range(parts - 1):
        terms.append(value.astype(bf16))
        value = value - terms[-1].astype(f32)
    return terms + [value.astype(bf16)]


def stacked_rows(values, width):
    at = lax.broadcasted_iota(jnp.int32, (16, width), 0)
    block = jnp.zeros((16, width), f32)
    for place, value in enumerate(values):
        block = jnp.where(at == place, value, block)
    return block.astype(bf16)


def pad_rows(blocks, width):
    depth = sum(block.shape[0] for block in blocks)
    short = -depth % 256
    return jnp.concatenate(blocks + ([jnp.zeros((short, width), bf16)] if short else []), axis=0)


def column_scale(inv_ref, emb):
    return jnp.broadcast_to(inv_ref[...], (128, emb)).T[:, :1]


def half_square(terms):
    value = sum(term.astype(f32) for term in terms)
    return 0.5 * jnp.sum(value * value, axis=0, keepdims=True)


def dot(x, y):
    return jnp.dot(x, y, preferred_element_type=f32)


def slab_kernel(width, slab_hbm, slab_probe_hbm, points_hbm, probes_hbm, inv_hbm, terms_ref, high_ref, low_ref,
                slab_ref, points_ref, inv_ref, slab_probe_ref, probes_ref, left, left_probe, total, sems):
    emb, rows = slab_ref.shape
    columns = [pl.ds(block * width, width) for block in range(points_ref.shape[1] // width)]
    pairs = [(inv_hbm, inv_ref), (slab_hbm, slab_ref), (slab_probe_hbm, slab_probe_ref)]
    pairs += [(points_hbm, points_ref), (probes_hbm, probes_ref)]
    arriving = [pltpu.make_async_copy(src, dst, sems.at[k]) for k, (src, dst) in enumerate(pairs)]
    for copy in arriving:
        copy.start()
    for copy in arriving[:3]:
        copy.wait()
    scale = column_scale(inv_ref, emb)
    slab = slab_ref[...] * scale
    u1, u2 = split(slab, 2)
    left[...] = jnp.concatenate([u1, u1, u2, u2], axis=0).T
    slab_square = jnp.broadcast_to(half_square((u1, u2)), (128, rows)).T[:, :1]
    p1, p2, p3 = split(slab_probe_ref[...], 3)
    left_probe[...] = pad_rows([p1, p1, p2, p1, p2, p3], rows).T
    for copy in arriving[3:]:
        copy.wait()
    one = jnp.ones((1, width), f32)
    for block, here in enumerate(columns):
        v1, v2, v3 = split(points_ref[:, here] * scale, 3)
        right = jnp.concatenate([v1, v2, v1, v2], axis=0)
        q1, q2, q3 = split(probes_ref[:, here], 3)
        right_probe = pad_rows([q1, q2, q1, q3, q2, q1], width)
        exponent = (dot(left[...], right) - slab_square) - half_square((v1, v2))
        weights = jnp.exp(exponent) * dot(left_probe[...], right_probe)
        high, low = split(weights, 2)
        high_ref[:, here] = high
        low_ref[:, here] = low
        both = jnp.concatenate([v1, v2, v3, stacked_rows([one], width)], axis=0)
        nt = (((1,), (1,)), ((), ()))
        part = lax.dot_general(high, both, nt, preferred_element_type=f32) + lax.dot_general(
            low, both, nt, preferred_element_type=f32
        )
        total[...] = part if block == 0 else total[...] + part
    sums = total[...].T
    mixed = sums[:emb] + (sums[emb : 2 * emb] + sums[2 * emb : 3 * emb])
    terms_ref[...] = -scale * (slab * sums[3 * emb : 3 * emb + 1] - mixed)


def slab_call(slab, slab_probe, points, probes, inv, width):
    emb, rows = slab.shape
    count = points.shape[1]
    operands = [pltpu.with_memory_space_constraint(v, pltpu.HBM) for v in (slab, slab_probe, points, probes, inv)]
    return pl.pallas_call(
        functools.partial(slab_kernel, width),
        out_shape=(
            pltpu.VMEM((emb, rows), f32),
            pltpu.VMEM((rows, count), bf16),
            pltpu.VMEM((rows, count), bf16),
            pltpu.VMEM(slab.shape, f32),
            pltpu.VMEM(points.shape, f32),
            pltpu.VMEM(inv.shape, f32),
        ),
        in_specs=[pl.BlockSpec(memory_space=pltpu.HBM)] * 5,
        out_specs=[pl.BlockSpec(memory_space=pltpu.VMEM)] * 6,
        scratch_shapes=[pltpu.VMEM(v.shape, f32) for v in (slab_probe, probes)]
        + [
            pltpu.VMEM((rows, 4 * emb), bf16),
            pltpu.VMEM((rows, 256), bf16),
            pltpu.VMEM((rows, 3 * emb + 16), f32),
            pltpu.SemaphoreType.DMA((5,)),
        ],
        compiler_params=pltpu.CompilerParams(vmem_limit_bytes=VMEM_LIMIT),
        cost_estimate=pl.CostEstimate(flops=7 * 10**9, bytes_accessed=5 * 10**6, transcendentals=rows * count),
        name="slab_terms",
    )(*operands)


def point_kernel(width, slab_ref, points_ref, inv_ref, high_ref, low_ref, terms_ref):
    emb, rows = slab_ref.shape
    scale = column_scale(inv_ref, emb)
    u1, u2, u3 = split(slab_ref[...] * scale, 3)
    left = jnp.concatenate([u1, u2, u3, stacked_rows([jnp.ones((1, rows), f32)], rows)], axis=0)
    for block in range(points_ref.shape[1] // width):
        columns = pl.ds(block * width, width)
        sums = dot(left, high_ref[:, columns]) + dot(left, low_ref[:, columns])
        mixed = sums[:emb] + (sums[emb : 2 * emb] + sums[2 * emb : 3 * emb])
        terms_ref[:, columns] = scale * (mixed - points_ref[:, columns] * scale * sums[3 * emb : 3 * emb + 1])


def point_call(slab, points, inv, high, low, width):
    rows, count = high.shape
    vmem = pl.BlockSpec(memory_space=pltpu.VMEM)
    return pl.pallas_call(
        functools.partial(point_kernel, width),
        out_shape=jax.ShapeDtypeStruct(points.shape, f32),
        in_specs=[vmem] * 5,
        out_specs=vmem,
        compiler_params=pltpu.CompilerParams(vmem_limit_bytes=VMEM_LIMIT),
        cost_estimate=pl.CostEstimate(flops=2 * 10**9, bytes_accessed=5 * 10**6, transcendentals=0),
        name="point_terms",
    )(slab, points, inv, high, low)


def sum_over(value, axis, size, beside=None):
    if size & (size - 1):
        return lax.psum(value, axis), beside
    steps = [1 << bit for bit in range(size.bit_length() - 1)]
    for place, step in enumerate(steps):
        other = lax.ppermute(value, axis, [(k, k ^ step) for k in range(size)])
        if place == len(steps) - 1 and beside is not None:
            other, beside = lax.optimization_barrier((other, beside))
        value = value + other
    return value, beside


def sum_over_columns(value, mesh, beside):
    size, others = mesh.shape["col"], mesh.shape["row"]
    if size & (size - 1):
        return lax.psum(value, "col"), beside
    bits = [1 << bit for bit in range(size.bit_length() - 1)]
    first = bits.pop(len(bits) // 2)
    even = [first] + bits
    odd = [even[k ^ 1] if k ^ 1 < len(even) else even[k] for k in range(len(even))]
    late = even[:-2] + even[:-3:-1] if len(even) > 3 else even
    for place in range(len(even)):
        pairs = [
            (col * others + row, (col ^ (odd if row % 2 else late if col & first else even)[place]) * others + row)
            for col in range(size)
            for row in range(others)
        ]
        other = lax.ppermute(value, ("col", "row"), pairs)
        if place == len(even) - 1:
            other, beside = lax.optimization_barrier((other, beside))
        value = value + other
    return value, beside


def solution(mesh):
    def local(slab_embed, slab_probe, point_embed, point_probe, inv_scale):
        inv = inv_scale.reshape(1, -1)
        width = 256 if point_embed.shape[1] % 256 == 0 else point_embed.shape[1]
        slab_terms, high, low, slab, points, scale = slab_call(slab_embed, slab_probe, point_embed, point_probe, inv, width)
        point_terms = point_call(slab, points, scale, high, low, width)
        point_grad, _ = sum_over(point_terms, "row", mesh.shape["row"])
        slab_grad, point_grad = sum_over_columns(slab_terms, mesh, point_grad)
        return slab_grad, point_grad

    placed = (P(None, "row"), P(None, "row"), P(None, "col"), P(None, "col"), P())
    return jax.shard_map(
        local, mesh=mesh, in_specs=placed, out_specs=(P(None, "row"), P(None, "col")), check_vma=False
    )
```

```python
import functools

import jax
import jax.numpy as jnp
from jax import lax
from jax.experimental import pallas as pl
from jax.experimental.pallas import tpu as pltpu
from jax.sharding import PartitionSpec as P

f32, bf16 = jnp.float32, jnp.bfloat16
VMEM_LIMIT = 40 * 2**20


def split(value, parts):
    terms = []
    for _ in range(parts - 1):
        terms.append(value.astype(bf16))
        value = value - terms[-1].astype(f32)
    return terms + [value.astype(bf16)]


def stacked_rows(values, width):
    at = lax.broadcasted_iota(jnp.int32, (16, width), 0)
    block = jnp.zeros((16, width), f32)
    for place, value in enumerate(values):
        block = jnp.where(at == place, value, block)
    return block.astype(bf16)


def pad_rows(blocks, width):
    depth = sum(block.shape[0] for block in blocks)
    short = -depth % 256
    return jnp.concatenate(blocks + ([jnp.zeros((short, width), bf16)] if short else []), axis=0)


def column_scale(inv_ref, emb):
    return jnp.broadcast_to(inv_ref[...], (128, emb)).T[:, :1]


def half_square(terms):
    value = sum(term.astype(f32) for term in terms)
    return 0.5 * jnp.sum(value * value, axis=0, keepdims=True)


def dot(x, y):
    return jnp.dot(x, y, preferred_element_type=f32)


def slab_kernel(width, slab_hbm, slab_probe_hbm, points_hbm, probes_hbm, inv_hbm, terms_ref, high_ref, low_ref,
                slab_ref, points_ref, inv_ref, slab_probe_ref, probes_ref, left, left_probe, total, sems):
    emb, rows = slab_ref.shape
    columns = [pl.ds(block * width, width) for block in range(points_ref.shape[1] // width)]
    pairs = [(inv_hbm, inv_ref), (slab_hbm, slab_ref), (slab_probe_hbm, slab_probe_ref)]
    pairs += [(points_hbm, points_ref), (probes_hbm, probes_ref)]
    arriving = [pltpu.make_async_copy(src, dst, sems.at[k]) for k, (src, dst) in enumerate(pairs)]
    for copy in arriving:
        copy.start()
    for copy in arriving[:3]:
        copy.wait()
    scale = column_scale(inv_ref, emb)
    slab = slab_ref[...] * scale
    u1, u2 = split(slab, 2)
    left[...] = jnp.concatenate([u1, u1, u2, u2], axis=0)
    slab_square = half_square((u1, u2))
    p1, p2, p3 = split(slab_probe_ref[...], 3)
    left_probe[...] = pad_rows([p1, p1, p1, p3, p2, p2], rows)
    for copy in arriving[3:]:
        copy.wait()
    one = jnp.ones((1, width), f32)
    for block, here in enumerate(columns):
        points = points_ref[:, here] * scale
        v1, v2, v3 = split(points, 3)
        point_square = jnp.broadcast_to(half_square((v1, v2)), (128, width)).T
        right = jnp.concatenate([v1, v2], axis=0).T
        right = jnp.concatenate([right, right], axis=1)
        q1, q2, q3 = split(probes_ref[:, here], 3)
        probe_rows = jnp.concatenate([q1, q2, q3, q1], axis=0).T
        probe_rows = jnp.concatenate([probe_rows, probe_rows], axis=1)
        exponent = (dot(right, left[...]) - slab_square) - jnp.concatenate([point_square] * (rows // 128), axis=1)
        weights = jnp.exp(exponent) * dot(probe_rows, left_probe[...])
        high, low = split(weights, 2)
        high_ref[here] = high
        low_ref[here] = low
        ones = stacked_rows([one], width)
        part = dot(jnp.concatenate([v1, v2, ones, v3], axis=0), high)
        part_low = dot(jnp.concatenate([v1, v2, ones], axis=0), low)
        both = jnp.concatenate([part[: 2 * emb + 16] + part_low, part[2 * emb + 16 :]], axis=0)
        total[...] = both if block == 0 else total[...] + both
    sums = total[...]
    mixed = sums[:emb] + (sums[emb : 2 * emb] + sums[2 * emb + 16 :])
    terms_ref[...] = -scale * (slab * sums[2 * emb : 2 * emb + 1] - mixed)


def slab_call(slab, slab_probe, points, probes, inv, width):
    emb, rows = slab.shape
    count = points.shape[1]
    operands = [pltpu.with_memory_space_constraint(v, pltpu.HBM) for v in (slab, slab_probe, points, probes, inv)]
    return pl.pallas_call(
        functools.partial(slab_kernel, width),
        out_shape=(
            pltpu.VMEM((emb, rows), f32),
            pltpu.VMEM((count, rows), bf16),
            pltpu.VMEM((count, rows), bf16),
            pltpu.VMEM(slab.shape, f32),
            pltpu.VMEM(points.shape, f32),
            pltpu.VMEM(inv.shape, f32),
        ),
        in_specs=[pl.BlockSpec(memory_space=pltpu.HBM)] * 5,
        out_specs=[pl.BlockSpec(memory_space=pltpu.VMEM)] * 6,
        scratch_shapes=[pltpu.VMEM(v.shape, f32) for v in (slab_probe, probes)]
        + [
            pltpu.VMEM((4 * emb, rows), bf16),
            pltpu.VMEM((256, rows), bf16),
            pltpu.VMEM((3 * emb + 16, rows), f32),
            pltpu.SemaphoreType.DMA((5,)),
        ],
        compiler_params=pltpu.CompilerParams(vmem_limit_bytes=VMEM_LIMIT),
        cost_estimate=pl.CostEstimate(flops=7 * 10**9, bytes_accessed=5 * 10**6, transcendentals=rows * count),
        name="slab_terms",
    )(*operands)


def point_kernel(width, slab_ref, points_ref, inv_ref, high_ref, low_ref, terms_ref):
    emb, rows = slab_ref.shape
    scale = column_scale(inv_ref, emb)
    u1, u2, u3 = split(slab_ref[...] * scale, 3)
    left = jnp.concatenate([u1, u2, u3, stacked_rows([jnp.ones((1, rows), f32)], rows)], axis=0)
    for block in range(points_ref.shape[1] // width):
        columns = pl.ds(block * width, width)
        nt = (((1,), (1,)), ((), ()))
        sums = lax.dot_general(left, high_ref[columns], nt, preferred_element_type=f32) + lax.dot_general(
            left, low_ref[columns], nt, preferred_element_type=f32
        )
        mixed = sums[:emb] + (sums[emb : 2 * emb] + sums[2 * emb : 3 * emb])
        terms_ref[:, columns] = scale * (mixed - points_ref[:, columns] * scale * sums[3 * emb : 3 * emb + 1])


def point_call(slab, points, inv, high, low, width):
    vmem = pl.BlockSpec(memory_space=pltpu.VMEM)
    return pl.pallas_call(
        functools.partial(point_kernel, width),
        out_shape=jax.ShapeDtypeStruct(points.shape, f32),
        in_specs=[vmem] * 5,
        out_specs=vmem,
        compiler_params=pltpu.CompilerParams(vmem_limit_bytes=VMEM_LIMIT),
        cost_estimate=pl.CostEstimate(flops=2 * 10**9, bytes_accessed=5 * 10**6, transcendentals=0),
        name="point_terms",
    )(slab, points, inv, high, low)


def sum_over(value, axis, size, beside=None):
    if size & (size - 1):
        return lax.psum(value, axis), beside
    steps = [1 << bit for bit in range(size.bit_length() - 1)]
    for place, step in enumerate(steps):
        other = lax.ppermute(value, axis, [(k, k ^ step) for k in range(size)])
        if place == len(steps) - 1 and beside is not None:
            other, beside = lax.optimization_barrier((other, beside))
        value = value + other
    return value, beside


def sum_over_columns(value, mesh, beside):
    size, others = mesh.shape["col"], mesh.shape["row"]
    if size & (size - 1):
        return lax.psum(value, "col"), beside
    bits = [1 << bit for bit in range(size.bit_length() - 1)]
    first = bits.pop(len(bits) // 2)
    even = [first] + bits
    odd = [even[k ^ 1] if k ^ 1 < len(even) else even[k] for k in range(len(even))]
    late = even[:-2] + even[:-3:-1] if len(even) > 3 else even
    for place in range(len(even)):
        pairs = [
            (col * others + row, (col ^ (odd if row % 2 else late if col & first else even)[place]) * others + row)
            for col in range(size)
            for row in range(others)
        ]
        other = lax.ppermute(value, ("col", "row"), pairs)
        if place == len(even) - 1:
            other, beside = lax.optimization_barrier((other, beside))
        value = value + other
    return value, beside


def solution(mesh):
    def local(slab_embed, slab_probe, point_embed, point_probe, inv_scale):
        inv = inv_scale.reshape(1, -1)
        width = 1024 if point_embed.shape[1] % 1024 == 0 else point_embed.shape[1]
        slab_terms, high, low, slab, points, scale = slab_call(slab_embed, slab_probe, point_embed, point_probe, inv, width)
        point_terms = point_call(slab, points, scale, high, low, width)
        point_grad, _ = sum_over(point_terms, "row", mesh.shape["row"])
        slab_grad, point_grad = sum_over_columns(slab_terms, mesh, point_grad)
        return slab_grad, point_grad

    placed = (P(None, "row"), P(None, "row"), P(None, "col"), P(None, "col"), P())
    return jax.shard_map(
        local, mesh=mesh, in_specs=placed, out_specs=(P(None, "row"), P(None, "col")), check_vma=False
    )
```

```python
import functools

import jax
import jax.numpy as jnp
from jax import lax
from jax.experimental import pallas as pl
from jax.experimental.pallas import tpu as pltpu
from jax.sharding import PartitionSpec as P

f32, bf16 = jnp.float32, jnp.bfloat16
VMEM_LIMIT = 40 * 2**20


def split(value, parts):
    terms = []
    for _ in range(parts - 1):
        terms.append(value.astype(bf16))
        value = value - terms[-1].astype(f32)
    return terms + [value.astype(bf16)]


def stacked_rows(values, width):
    at = lax.broadcasted_iota(jnp.int32, (16, width), 0)
    block = jnp.zeros((16, width), f32)
    for place, value in enumerate(values):
        block = jnp.where(at == place, value, block)
    return block.astype(bf16)


def pad_rows(blocks, width):
    depth = sum(block.shape[0] for block in blocks)
    short = -depth % 256
    return jnp.concatenate(blocks + ([jnp.zeros((short, width), bf16)] if short else []), axis=0)


def column_scale(inv_ref, emb):
    return jnp.broadcast_to(inv_ref[...], (128, emb)).T[:, :1]


def half_square(terms):
    value = sum(term.astype(f32) for term in terms)
    return 0.5 * jnp.sum(value * value, axis=0, keepdims=True)


def dot(x, y):
    return jnp.dot(x, y, preferred_element_type=f32)


def slab_kernel(width, slab_hbm, slab_probe_hbm, points_hbm, probes_hbm, inv_hbm, terms_ref, high_ref, low_ref,
                slab_ref, points_ref, inv_ref, slab_probe_ref, probes_ref, left, left_probe, total, sems):
    emb, rows = slab_ref.shape
    columns = [pl.ds(block * width, width) for block in range(points_ref.shape[1] // width)]
    pairs = [(inv_hbm, inv_ref), (slab_hbm, slab_ref), (slab_probe_hbm, slab_probe_ref)]
    pairs += [(points_hbm, points_ref), (probes_hbm, probes_ref)]
    arriving = [pltpu.make_async_copy(src, dst, sems.at[k]) for k, (src, dst) in enumerate(pairs)]
    for copy in arriving:
        copy.start()
    for copy in arriving[:3]:
        copy.wait()
    scale = column_scale(inv_ref, emb)
    slab = slab_ref[...] * scale
    u1, u2 = split(slab, 2)
    left[...] = jnp.concatenate([u1, u1, u2, u2], axis=0)
    slab_square = half_square((u1, u2))
    p1, p2, p3 = split(slab_probe_ref[...], 3)
    left_probe[...] = pad_rows([p1, p1, p1, p3, p2, p2], rows)
    for copy in arriving[3:]:
        copy.wait()
    one = jnp.ones((1, width), f32)
    for block, here in enumerate(columns):
        points = points_ref[:, here] * scale
        v1, v2, v3 = split(points, 3)
        point_square = jnp.broadcast_to(half_square((v1, v2)), (128, width)).T
        right = jnp.concatenate([v1, v2], axis=0).T
        right = jnp.concatenate([right, right], axis=1)
        q1, q2, q3 = split(probes_ref[:, here], 3)
        probe_rows = jnp.concatenate([q1, q2, q3, q1], axis=0).T
        probe_rows = jnp.concatenate([probe_rows, probe_rows], axis=1)
        exponent = (dot(right, left[...]) - slab_square) - jnp.concatenate([point_square] * (rows // 128), axis=1)
        weights = jnp.exp(exponent) * dot(probe_rows, left_probe[...])
        high, low = split(weights, 2)
        high_ref[here] = high
        low_ref[here] = low
        high, low = high_ref[here], low_ref[here]
        ones = stacked_rows([one], width)
        part = dot(jnp.concatenate([v1, v2, ones, v3], axis=0), high)
        part_low = dot(jnp.concatenate([v1, v2, ones], axis=0), low)
        both = jnp.concatenate([part[: 2 * emb + 16] + part_low, part[2 * emb + 16 :]], axis=0)
        total[...] = both if block == 0 else total[...] + both
    sums = total[...]
    mixed = sums[:emb] + (sums[emb : 2 * emb] + sums[2 * emb + 16 :])
    terms_ref[...] = -scale * (slab * sums[2 * emb : 2 * emb + 1] - mixed)


def slab_call(slab, slab_probe, points, probes, inv, width):
    emb, rows = slab.shape
    count = points.shape[1]
    operands = [pltpu.with_memory_space_constraint(v, pltpu.HBM) for v in (slab, slab_probe, points, probes, inv)]
    return pl.pallas_call(
        functools.partial(slab_kernel, width),
        out_shape=(
            pltpu.VMEM((emb, rows), f32),
            pltpu.VMEM((count, rows), bf16),
            pltpu.VMEM((count, rows), bf16),
            pltpu.VMEM(slab.shape, f32),
            pltpu.VMEM(points.shape, f32),
            pltpu.VMEM(inv.shape, f32),
        ),
        in_specs=[pl.BlockSpec(memory_space=pltpu.HBM)] * 5,
        out_specs=[pl.BlockSpec(memory_space=pltpu.VMEM)] * 6,
        scratch_shapes=[pltpu.VMEM(v.shape, f32) for v in (slab_probe, probes)]
        + [
            pltpu.VMEM((4 * emb, rows), bf16),
            pltpu.VMEM((256, rows), bf16),
            pltpu.VMEM((3 * emb + 16, rows), f32),
            pltpu.SemaphoreType.DMA((5,)),
        ],
        compiler_params=pltpu.CompilerParams(vmem_limit_bytes=VMEM_LIMIT),
        cost_estimate=pl.CostEstimate(flops=7 * 10**9, bytes_accessed=5 * 10**6, transcendentals=rows * count),
        name="slab_terms",
    )(*operands)


def point_kernel(width, slab_ref, points_ref, inv_ref, high_ref, low_ref, terms_ref):
    emb, rows = slab_ref.shape
    scale = column_scale(inv_ref, emb)
    u1, u2, u3 = split(slab_ref[...] * scale, 3)
    left = jnp.concatenate([u1, u2, u3, stacked_rows([jnp.ones((1, rows), f32)], rows)], axis=0)
    for block in range(points_ref.shape[1] // width):
        columns = pl.ds(block * width, width)
        nt = (((1,), (1,)), ((), ()))
        sums = lax.dot_general(left, high_ref[columns], nt, preferred_element_type=f32) + lax.dot_general(
            left, low_ref[columns], nt, preferred_element_type=f32
        )
        mixed = sums[:emb] + (sums[emb : 2 * emb] + sums[2 * emb : 3 * emb])
        terms_ref[:, columns] = scale * (mixed - points_ref[:, columns] * scale * sums[3 * emb : 3 * emb + 1])


def point_call(slab, points, inv, high, low, width):
    vmem = pl.BlockSpec(memory_space=pltpu.VMEM)
    return pl.pallas_call(
        functools.partial(point_kernel, width),
        out_shape=jax.ShapeDtypeStruct(points.shape, f32),
        in_specs=[vmem] * 5,
        out_specs=vmem,
        compiler_params=pltpu.CompilerParams(vmem_limit_bytes=VMEM_LIMIT),
        cost_estimate=pl.CostEstimate(flops=2 * 10**9, bytes_accessed=5 * 10**6, transcendentals=0),
        name="point_terms",
    )(slab, points, inv, high, low)


def sum_over(value, axis, size, beside=None):
    if size & (size - 1):
        return lax.psum(value, axis), beside
    steps = [1 << bit for bit in range(size.bit_length() - 1)]
    for place, step in enumerate(steps):
        other = lax.ppermute(value, axis, [(k, k ^ step) for k in range(size)])
        if place == len(steps) - 1 and beside is not None:
            other, beside = lax.optimization_barrier((other, beside))
        value = value + other
    return value, beside


def sum_over_columns(value, mesh, beside):
    size, others = mesh.shape["col"], mesh.shape["row"]
    if size & (size - 1):
        return lax.psum(value, "col"), beside
    bits = [1 << bit for bit in range(size.bit_length() - 1)]
    first = bits.pop(len(bits) // 2)
    even, odd = [first] + bits, bits[:1] + [first] + bits[1:]
    orders = {0: (even, odd), first: (even, odd)}
    if len(bits) > 2:
        orders[first] = [first] + bits[-1:] + bits[:-1], bits[:1] + [first] + bits[-1:] + bits[1:-1]
    for place in range(len(even)):
        pairs = [
            (col * others + row, (col ^ orders[col & first][row % 2][place]) * others + row)
            for col in range(size)
            for row in range(others)
        ]
        other = lax.ppermute(value, ("col", "row"), pairs)
        if place == len(even) - 1:
            other, beside = lax.optimization_barrier((other, beside))
        value = value + other
    return value, beside


def solution(mesh):
    def local(slab_embed, slab_probe, point_embed, point_probe, inv_scale):
        inv = inv_scale.reshape(1, -1)
        width = 1024 if point_embed.shape[1] % 1024 == 0 else point_embed.shape[1]
        slab_terms, high, low, slab, points, scale = slab_call(slab_embed, slab_probe, point_embed, point_probe, inv, width)
        point_terms = point_call(slab, points, scale, high, low, width)
        point_grad, _ = sum_over(point_terms, "row", mesh.shape["row"])
        slab_grad, point_grad = sum_over_columns(slab_terms, mesh, point_grad)
        return slab_grad, point_grad

    placed = (P(None, "row"), P(None, "row"), P(None, "col"), P(None, "col"), P())
    return jax.shard_map(
        local, mesh=mesh, in_specs=placed, out_specs=(P(None, "row"), P(None, "col")), check_vma=False
    )
```

```python
import functools

import jax
import jax.numpy as jnp
from jax import lax
from jax.experimental import pallas as pl
from jax.experimental.pallas import tpu as pltpu
from jax.sharding import PartitionSpec as P

f32, bf16 = jnp.float32, jnp.bfloat16
VMEM_LIMIT = 40 * 2**20


def split(value, parts):
    terms = []
    for _ in range(parts - 1):
        terms.append(value.astype(bf16))
        value = value - terms[-1].astype(f32)
    return terms + [value.astype(bf16)]


def stacked_rows(values, width):
    at = lax.broadcasted_iota(jnp.int32, (16, width), 0)
    block = jnp.zeros((16, width), f32)
    for place, value in enumerate(values):
        block = jnp.where(at == place, value, block)
    return block.astype(bf16)


def pad_rows(blocks, width):
    depth = sum(block.shape[0] for block in blocks)
    short = -depth % 256
    return jnp.concatenate(blocks + ([jnp.zeros((short, width), bf16)] if short else []), axis=0)


def column_scale(inv_ref, emb):
    return jnp.broadcast_to(inv_ref[...], (128, emb)).T[:, :1]


def half_square(terms):
    value = sum(term.astype(f32) for term in terms)
    return 0.5 * jnp.sum(value * value, axis=0, keepdims=True)


def dot(x, y):
    return jnp.dot(x, y, preferred_element_type=f32)


def slab_kernel(width, slab_hbm, slab_probe_hbm, points_hbm, probes_hbm, inv_hbm, terms_ref, high_ref, low_ref,
                slab_ref, points_ref, inv_ref, slab_probe_ref, probes_ref, left, left_probe, total, sems):
    emb, rows = slab_ref.shape
    columns = [pl.ds(block * width, width) for block in range(points_ref.shape[1] // width)]
    pairs = [(inv_hbm, inv_ref), (slab_hbm, slab_ref), (slab_probe_hbm, slab_probe_ref)]
    pairs += [(points_hbm, points_ref), (probes_hbm, probes_ref)]
    arriving = [pltpu.make_async_copy(src, dst, sems.at[k]) for k, (src, dst) in enumerate(pairs)]
    for copy in arriving:
        copy.start()
    for copy in arriving[:3]:
        copy.wait()
    scale = column_scale(inv_ref, emb)
    slab = slab_ref[...] * scale
    u1, u2 = split(slab, 2)
    left[...] = jnp.concatenate([u1, u1, u2, u2], axis=0)
    slab_square = half_square((u1, u2))
    p1, p2, p3 = split(slab_probe_ref[...], 3)
    left_probe[...] = pad_rows([p1, p1, p1, p3, p2, p2], rows)
    for copy in arriving[3:]:
        copy.wait()
    one = jnp.ones((1, width), f32)
    for block, here in enumerate(columns):
        points = points_ref[:, here] * scale
        v1, v2, v3 = split(points, 3)
        point_square = jnp.broadcast_to(half_square((v1, v2)), (128, width)).T
        right = jnp.concatenate([v1, v2], axis=0).T
        right = jnp.concatenate([right, right], axis=1)
        q1, q2, q3 = split(probes_ref[:, here], 3)
        probe_rows = jnp.concatenate([q1, q2, q3, q1], axis=0).T
        probe_rows = jnp.concatenate([probe_rows, probe_rows], axis=1)
        for start in range(0, width, 512):
            some = slice(start, start + 512)
            exponent = (dot(right[some], left[...]) - slab_square) - jnp.concatenate([point_square[some]] * (rows // 128), axis=1)
            weights = jnp.exp(exponent) * dot(probe_rows[some], left_probe[...])
            high, low = split(weights, 2)
            at = pl.ds(block * width + start, 512)
            high_ref[at] = high
            low_ref[at] = low
        high, low = high_ref[here], low_ref[here]
        ones = stacked_rows([one], width)
        part = dot(jnp.concatenate([v1, v2, ones, v3], axis=0), high)
        part_low = dot(jnp.concatenate([v1, v2, ones], axis=0), low)
        both = jnp.concatenate([part[: 2 * emb + 16] + part_low, part[2 * emb + 16 :]], axis=0)
        total[...] = both if block == 0 else total[...] + both
    sums = total[...]
    mixed = sums[:emb] + (sums[emb : 2 * emb] + sums[2 * emb + 16 :])
    terms_ref[...] = -scale * (slab * sums[2 * emb : 2 * emb + 1] - mixed)


def slab_call(slab, slab_probe, points, probes, inv, width):
    emb, rows = slab.shape
    count = points.shape[1]
    operands = [pltpu.with_memory_space_constraint(v, pltpu.HBM) for v in (slab, slab_probe, points, probes, inv)]
    return pl.pallas_call(
        functools.partial(slab_kernel, width),
        out_shape=(
            pltpu.VMEM((emb, rows), f32),
            pltpu.VMEM((count, rows), bf16),
            pltpu.VMEM((count, rows), bf16),
            pltpu.VMEM(slab.shape, f32),
            pltpu.VMEM(points.shape, f32),
            pltpu.VMEM(inv.shape, f32),
        ),
        in_specs=[pl.BlockSpec(memory_space=pltpu.HBM)] * 5,
        out_specs=[pl.BlockSpec(memory_space=pltpu.VMEM)] * 6,
        scratch_shapes=[pltpu.VMEM(v.shape, f32) for v in (slab_probe, probes)]
        + [
            pltpu.VMEM((4 * emb, rows), bf16),
            pltpu.VMEM((256, rows), bf16),
            pltpu.VMEM((3 * emb + 16, rows), f32),
            pltpu.SemaphoreType.DMA((5,)),
        ],
        compiler_params=pltpu.CompilerParams(vmem_limit_bytes=VMEM_LIMIT),
        cost_estimate=pl.CostEstimate(flops=7 * 10**9, bytes_accessed=5 * 10**6, transcendentals=rows * count),
        name="slab_terms",
    )(*operands)


def point_kernel(width, slab_ref, points_ref, inv_ref, high_ref, low_ref, terms_ref):
    emb, rows = slab_ref.shape
    scale = column_scale(inv_ref, emb)
    u1, u2, u3 = split(slab_ref[...] * scale, 3)
    left = jnp.concatenate([u1, u2, u3, stacked_rows([jnp.ones((1, rows), f32)], rows)], axis=0)
    for block in range(points_ref.shape[1] // width):
        columns = pl.ds(block * width, width)
        nt = (((1,), (1,)), ((), ()))
        sums = lax.dot_general(left, high_ref[columns], nt, preferred_element_type=f32) + lax.dot_general(
            left, low_ref[columns], nt, preferred_element_type=f32
        )
        mixed = sums[:emb] + (sums[emb : 2 * emb] + sums[2 * emb : 3 * emb])
        terms_ref[:, columns] = scale * (mixed - points_ref[:, columns] * scale * sums[3 * emb : 3 * emb + 1])


def point_call(slab, points, inv, high, low, width):
    vmem = pl.BlockSpec(memory_space=pltpu.VMEM)
    return pl.pallas_call(
        functools.partial(point_kernel, width),
        out_shape=jax.ShapeDtypeStruct(points.shape, f32),
        in_specs=[vmem] * 5,
        out_specs=vmem,
        compiler_params=pltpu.CompilerParams(vmem_limit_bytes=VMEM_LIMIT),
        cost_estimate=pl.CostEstimate(flops=2 * 10**9, bytes_accessed=5 * 10**6, transcendentals=0),
        name="point_terms",
    )(slab, points, inv, high, low)


def sum_over(value, axis, size, beside=None):
    if size & (size - 1):
        return lax.psum(value, axis), beside
    steps = [1 << bit for bit in range(size.bit_length() - 1)]
    for place, step in enumerate(steps):
        other = lax.ppermute(value, axis, [(k, k ^ step) for k in range(size)])
        if place == len(steps) - 1 and beside is not None:
            other, beside = lax.optimization_barrier((other, beside))
        value = value + other
    return value, beside


def sum_over_columns(value, mesh, beside):
    size, others = mesh.shape["col"], mesh.shape["row"]
    if size & (size - 1):
        return lax.psum(value, "col"), beside
    bits = [1 << bit for bit in range(size.bit_length() - 1)]
    first = bits.pop(len(bits) // 2)
    even, odd = [first] + bits, bits[:1] + [first] + bits[1:]
    orders = {0: (even, odd), first: (even, odd)}
    if len(bits) > 2:
        orders[first] = [first] + bits[-1:] + bits[:-1], bits[:1] + [first] + bits[-1:] + bits[1:-1]
    for place in range(len(even)):
        pairs = [
            (col * others + row, (col ^ orders[col & first][row % 2][place]) * others + row)
            for col in range(size)
            for row in range(others)
        ]
        other = lax.ppermute(value, ("col", "row"), pairs)
        if place == len(even) - 1:
            other, beside = lax.optimization_barrier((other, beside))
        value = value + other
    return value, beside


def solution(mesh):
    def local(slab_embed, slab_probe, point_embed, point_probe, inv_scale):
        inv = inv_scale.reshape(1, -1)
        width = 1024 if point_embed.shape[1] % 1024 == 0 else point_embed.shape[1]
        slab_terms, high, low, slab, points, scale = slab_call(slab_embed, slab_probe, point_embed, point_probe, inv, width)
        point_terms = point_call(slab, points, scale, high, low, width // 2)
        point_grad, _ = sum_over(point_terms, "row", mesh.shape["row"])
        slab_grad, point_grad = sum_over_columns(slab_terms, mesh, point_grad)
        return slab_grad, point_grad

    placed = (P(None, "row"), P(None, "row"), P(None, "col"), P(None, "col"), P())
    return jax.shard_map(
        local, mesh=mesh, in_specs=placed, out_specs=(P(None, "row"), P(None, "col")), check_vma=False
    )
```

```python
import functools

import jax
import jax.numpy as jnp
from jax import lax
from jax.experimental import pallas as pl
from jax.experimental.pallas import tpu as pltpu
from jax.sharding import PartitionSpec as P

f32, bf16 = jnp.float32, jnp.bfloat16
VMEM_LIMIT = 40 * 2**20


def split(value, parts):
    terms = []
    for _ in range(parts - 1):
        terms.append(value.astype(bf16))
        value = value - terms[-1].astype(f32)
    return terms + [value.astype(bf16)]


def stacked_rows(values, width):
    at = lax.broadcasted_iota(jnp.int32, (16, width), 0)
    block = jnp.zeros((16, width), f32)
    for place, value in enumerate(values):
        block = jnp.where(at == place, value, block)
    return block.astype(bf16)


def pad_rows(blocks, width):
    depth = sum(block.shape[0] for block in blocks)
    short = -depth % 256
    return jnp.concatenate(blocks + ([jnp.zeros((short, width), bf16)] if short else []), axis=0)


def column_scale(inv_ref, emb):
    return jnp.broadcast_to(inv_ref[...], (128, emb)).T[:, :1]


def half_square(terms):
    value = sum(term.astype(f32) for term in terms)
    return 0.5 * jnp.sum(value * value, axis=0, keepdims=True)


def dot(x, y):
    return jnp.dot(x, y, preferred_element_type=f32)


def slab_kernel(width, slab_hbm, slab_probe_hbm, points_hbm, probes_hbm, inv_hbm, terms_ref, high_ref, low_ref,
                slab_ref, points_ref, inv_ref, slab_probe_ref, probes_ref, left, left_probe, total, sems):
    emb, rows = slab_ref.shape
    columns = [pl.ds(block * width, width) for block in range(points_ref.shape[1] // width)]
    pairs = [(inv_hbm, inv_ref), (slab_hbm, slab_ref), (slab_probe_hbm, slab_probe_ref)]
    pairs += [(points_hbm, points_ref), (probes_hbm, probes_ref)]
    arriving = [pltpu.make_async_copy(src, dst, sems.at[k]) for k, (src, dst) in enumerate(pairs)]
    for copy in arriving:
        copy.start()
    for copy in arriving[:3]:
        copy.wait()
    scale = column_scale(inv_ref, emb)
    slab = slab_ref[...] * scale
    u1, u2 = split(slab, 2)
    left[...] = jnp.concatenate([u1, u1, u2, u2], axis=0)
    slab_square = half_square((u1, u2))
    p1, p2, p3 = split(slab_probe_ref[...], 3)
    left_probe[...] = pad_rows([p1, p1, p1, p3, p2, p2], rows)
    for copy in arriving[3:]:
        copy.wait()
    one = jnp.ones((1, width), f32)
    for block, here in enumerate(columns):
        points = points_ref[:, here] * scale
        v1, v2, v3 = split(points, 3)
        point_square = jnp.broadcast_to(half_square((v1, v2)), (128, width)).T
        right = jnp.concatenate([v1, v2], axis=0).T
        right = jnp.concatenate([right, right], axis=1)
        q1, q2, q3 = split(probes_ref[:, here], 3)
        probe_rows = jnp.concatenate([q1, q2, q3, q1], axis=0).T
        probe_rows = jnp.concatenate([probe_rows, probe_rows], axis=1)
        exponent = (dot(right, left[...]) - slab_square) - jnp.concatenate([point_square] * (rows // 128), axis=1)
        weights = jnp.exp(exponent) * dot(probe_rows, left_probe[...])
        high, low = split(weights, 2)
        high_ref[here] = high
        low_ref[here] = low
        high, low = high_ref[here], low_ref[here]
        ones = stacked_rows([one], width)
        part = dot(jnp.concatenate([v1, v2, ones, v3], axis=0), high)
        part_low = dot(jnp.concatenate([v1, v2, ones], axis=0), low)
        both = jnp.concatenate([part[: 2 * emb + 16] + part_low, part[2 * emb + 16 :]], axis=0)
        total[...] = both if block == 0 else total[...] + both
    sums = total[...]
    mixed = sums[:emb] + (sums[emb : 2 * emb] + sums[2 * emb + 16 :])
    terms_ref[...] = -scale * (slab * sums[2 * emb : 2 * emb + 1] - mixed)


def slab_call(slab, slab_probe, points, probes, inv, width):
    emb, rows = slab.shape
    count = points.shape[1]
    operands = [pltpu.with_memory_space_constraint(v, pltpu.HBM) for v in (slab, slab_probe, points, probes, inv)]
    return pl.pallas_call(
        functools.partial(slab_kernel, width),
        out_shape=(
            pltpu.VMEM((emb, rows), f32),
            pltpu.VMEM((count, rows), bf16),
            pltpu.VMEM((count, rows), bf16),
            pltpu.VMEM(slab.shape, f32),
            pltpu.VMEM(points.shape, f32),
            pltpu.VMEM(inv.shape, f32),
        ),
        in_specs=[pl.BlockSpec(memory_space=pltpu.HBM)] * 5,
        out_specs=[pl.BlockSpec(memory_space=pltpu.VMEM)] * 6,
        scratch_shapes=[pltpu.VMEM(v.shape, f32) for v in (slab_probe, probes)]
        + [
            pltpu.VMEM((4 * emb, rows), bf16),
            pltpu.VMEM((256, rows), bf16),
            pltpu.VMEM((3 * emb + 16, rows), f32),
            pltpu.SemaphoreType.DMA((5,)),
        ],
        compiler_params=pltpu.CompilerParams(vmem_limit_bytes=VMEM_LIMIT),
        cost_estimate=pl.CostEstimate(flops=7 * 10**9, bytes_accessed=5 * 10**6, transcendentals=rows * count),
        name="slab_terms",
    )(*operands)


def point_kernel(width, slab_ref, points_ref, inv_ref, high_ref, low_ref, terms_ref):
    emb, rows = slab_ref.shape
    scale = column_scale(inv_ref, emb)
    u1, u2, u3 = split(slab_ref[...] * scale, 3)
    left = jnp.concatenate([u1, u2, u3, stacked_rows([jnp.ones((1, rows), f32)], rows)], axis=0)
    for block in range(points_ref.shape[1] // width):
        columns = pl.ds(block * width, width)
        nt = (((1,), (1,)), ((), ()))
        sums = lax.dot_general(left, high_ref[columns], nt, preferred_element_type=f32) + lax.dot_general(
            left, low_ref[columns], nt, preferred_element_type=f32
        )
        mixed = sums[:emb] + (sums[emb : 2 * emb] + sums[2 * emb : 3 * emb])
        terms_ref[:, columns] = scale * (mixed - points_ref[:, columns] * scale * sums[3 * emb : 3 * emb + 1])


def point_call(slab, points, inv, high, low, width):
    vmem = pl.BlockSpec(memory_space=pltpu.VMEM)
    return pl.pallas_call(
        functools.partial(point_kernel, width),
        out_shape=jax.ShapeDtypeStruct(points.shape, f32),
        in_specs=[vmem] * 5,
        out_specs=vmem,
        compiler_params=pltpu.CompilerParams(vmem_limit_bytes=VMEM_LIMIT),
        cost_estimate=pl.CostEstimate(flops=2 * 10**9, bytes_accessed=5 * 10**6, transcendentals=0),
        name="point_terms",
    )(slab, points, inv, high, low)


def sum_over(value, axis, size, beside=None):
    if size & (size - 1):
        return lax.psum(value, axis), beside
    steps = [1 << bit for bit in range(size.bit_length() - 1)]
    for place, step in enumerate(steps):
        other = lax.ppermute(value, axis, [(k, k ^ step) for k in range(size)])
        if place == len(steps) - 1 and beside is not None:
            other, beside = lax.optimization_barrier((other, beside))
        value = value + other
    return value, beside


def sum_over_columns(value, mesh, beside):
    size, others = mesh.shape["col"], mesh.shape["row"]
    if size & (size - 1):
        return lax.psum(value, "col"), beside
    bits = [1 << bit for bit in range(size.bit_length() - 1)]
    first = bits.pop(len(bits) // 2)
    even, odd = [first] + bits, bits[:1] + [first] + bits[1:]
    orders = {0: (even, odd), first: (even, odd)}
    if len(bits) > 2:
        orders[first] = [first] + bits[-1:] + bits[:-1], odd
    for place in range(len(even)):
        pairs = [
            (col * others + row, (col ^ orders[col & first][row % 2][place]) * others + row)
            for col in range(size)
            for row in range(others)
        ]
        other = lax.ppermute(value, ("col", "row"), pairs)
        if place == len(even) - 1:
            other, beside = lax.optimization_barrier((other, beside))
        value = value + other
    return value, beside


def solution(mesh):
    def local(slab_embed, slab_probe, point_embed, point_probe, inv_scale):
        inv = inv_scale.reshape(1, -1)
        width = 1024 if point_embed.shape[1] % 1024 == 0 else point_embed.shape[1]
        slab_terms, high, low, slab, points, scale = slab_call(slab_embed, slab_probe, point_embed, point_probe, inv, width)
        point_terms = point_call(slab, points, scale, high, low, width // 2)
        point_grad, _ = sum_over(point_terms, "row", mesh.shape["row"])
        slab_grad, point_grad = sum_over_columns(slab_terms, mesh, point_grad)
        return slab_grad, point_grad

    placed = (P(None, "row"), P(None, "row"), P(None, "col"), P(None, "col"), P())
    return jax.shard_map(
        local, mesh=mesh, in_specs=placed, out_specs=(P(None, "row"), P(None, "col")), check_vma=False
    )
```

```python
import functools

import jax
import jax.numpy as jnp
from jax import lax
from jax.experimental import pallas as pl
from jax.experimental.pallas import tpu as pltpu
from jax.sharding import PartitionSpec as P

f32, bf16 = jnp.float32, jnp.bfloat16
VMEM_LIMIT = 40 * 2**20


def split(value, parts):
    terms = []
    for _ in range(parts - 1):
        terms.append(value.astype(bf16))
        value = value - terms[-1].astype(f32)
    return terms + [value.astype(bf16)]


def stacked_rows(values, width):
    at = lax.broadcasted_iota(jnp.int32, (16, width), 0)
    block = jnp.zeros((16, width), f32)
    for place, value in enumerate(values):
        block = jnp.where(at == place, value, block)
    return block.astype(bf16)


def pad_rows(blocks, width):
    depth = sum(block.shape[0] for block in blocks)
    short = -depth % 256
    return jnp.concatenate(blocks + ([jnp.zeros((short, width), bf16)] if short else []), axis=0)


def column_scale(inv_ref, emb):
    return jnp.broadcast_to(inv_ref[...], (128, emb)).T[:, :1]


def half_square(terms):
    value = sum(term.astype(f32) for term in terms)
    return 0.5 * jnp.sum(value * value, axis=0, keepdims=True)


def dot(x, y):
    return jnp.dot(x, y, preferred_element_type=f32)


def slab_kernel(width, slab_hbm, slab_probe_hbm, points_hbm, probes_hbm, inv_hbm, terms_ref, high_ref, low_ref,
                slab_ref, points_ref, inv_ref, slab_probe_ref, probes_ref, left, left_probe, total, sems):
    emb, rows = slab_ref.shape
    columns = [pl.ds(block * width, width) for block in range(points_ref.shape[1] // width)]
    pairs = [(inv_hbm, inv_ref), (slab_hbm, slab_ref), (slab_probe_hbm, slab_probe_ref)]
    pairs += [(points_hbm, points_ref), (probes_hbm, probes_ref)]
    arriving = [pltpu.make_async_copy(src, dst, sems.at[k]) for k, (src, dst) in enumerate(pairs)]
    for copy in arriving:
        copy.start()
    for copy in arriving[:3]:
        copy.wait()
    scale = column_scale(inv_ref, emb)
    slab = slab_ref[...] * scale
    u1, u2 = split(slab, 2)
    left[...] = jnp.concatenate([u1, u1, u2, u2], axis=0)
    slab_square = half_square((u1, u2))
    p1, p2, p3 = split(slab_probe_ref[...], 3)
    left_probe[...] = pad_rows([p1, p1, p1, p3, p2, p2], rows)
    for copy in arriving[3:]:
        copy.wait()
    one = jnp.ones((1, width), f32)
    for block, here in enumerate(columns):
        points = points_ref[:, here] * scale
        v1, v2, v3 = split(points, 3)
        point_square = jnp.broadcast_to(half_square((v1, v2)), (128, width)).T
        right = jnp.concatenate([v1, v2], axis=0).T
        right = jnp.concatenate([right, right], axis=1)
        q1, q2, q3 = split(probes_ref[:, here], 3)
        probe_rows = jnp.concatenate([q1, q2, q3, q1], axis=0).T
        probe_rows = jnp.concatenate([probe_rows, probe_rows], axis=1)
        for start in range(0, width, 256):
            some = slice(start, start + 256)
            exponent = (dot(right[some], left[...]) - slab_square) - jnp.concatenate([point_square[some]] * (rows // 128), axis=1)
            weights = jnp.exp(exponent) * dot(probe_rows[some], left_probe[...])
            high, low = split(weights, 2)
            at = pl.ds(block * width + start, 256)
            high_ref[at] = high
            low_ref[at] = low
        high, low = high_ref[here], low_ref[here]
        ones = stacked_rows([one], width)
        part = dot(jnp.concatenate([v1, v2, ones, v3], axis=0), high)
        part_low = dot(jnp.concatenate([v1, v2, ones], axis=0), low)
        both = jnp.concatenate([part[: 2 * emb + 16] + part_low, part[2 * emb + 16 :]], axis=0)
        total[...] = both if block == 0 else total[...] + both
    sums = total[...]
    mixed = sums[:emb] + (sums[emb : 2 * emb] + sums[2 * emb + 16 :])
    terms_ref[...] = -scale * (slab * sums[2 * emb : 2 * emb + 1] - mixed)


def slab_call(slab, slab_probe, points, probes, inv, width):
    emb, rows = slab.shape
    count = points.shape[1]
    operands = [pltpu.with_memory_space_constraint(v, pltpu.HBM) for v in (slab, slab_probe, points, probes, inv)]
    return pl.pallas_call(
        functools.partial(slab_kernel, width),
        out_shape=(
            pltpu.VMEM((emb, rows), f32),
            pltpu.VMEM((count, rows), bf16),
            pltpu.VMEM((count, rows), bf16),
            pltpu.VMEM(slab.shape, f32),
            pltpu.VMEM(points.shape, f32),
            pltpu.VMEM(inv.shape, f32),
        ),
        in_specs=[pl.BlockSpec(memory_space=pltpu.HBM)] * 5,
        out_specs=[pl.BlockSpec(memory_space=pltpu.VMEM)] * 6,
        scratch_shapes=[pltpu.VMEM(v.shape, f32) for v in (slab_probe, probes)]
        + [
            pltpu.VMEM((4 * emb, rows), bf16),
            pltpu.VMEM((256, rows), bf16),
            pltpu.VMEM((3 * emb + 16, rows), f32),
            pltpu.SemaphoreType.DMA((5,)),
        ],
        compiler_params=pltpu.CompilerParams(vmem_limit_bytes=VMEM_LIMIT),
        cost_estimate=pl.CostEstimate(flops=7 * 10**9, bytes_accessed=5 * 10**6, transcendentals=rows * count),
        name="slab_terms",
    )(*operands)


def point_kernel(width, slab_ref, points_ref, inv_ref, high_ref, low_ref, terms_ref):
    emb, rows = slab_ref.shape
    scale = column_scale(inv_ref, emb)
    u1, u2, u3 = split(slab_ref[...] * scale, 3)
    left = jnp.concatenate([u1, u2, u3, stacked_rows([jnp.ones((1, rows), f32)], rows)], axis=0)
    for block in range(points_ref.shape[1] // width):
        columns = pl.ds(block * width, width)
        nt = (((1,), (1,)), ((), ()))
        sums = lax.dot_general(left, high_ref[columns], nt, preferred_element_type=f32) + lax.dot_general(
            left, low_ref[columns], nt, preferred_element_type=f32
        )
        mixed = sums[:emb] + (sums[emb : 2 * emb] + sums[2 * emb : 3 * emb])
        terms_ref[:, columns] = scale * (mixed - points_ref[:, columns] * scale * sums[3 * emb : 3 * emb + 1])


def point_call(slab, points, inv, high, low, width):
    vmem = pl.BlockSpec(memory_space=pltpu.VMEM)
    return pl.pallas_call(
        functools.partial(point_kernel, width),
        out_shape=jax.ShapeDtypeStruct(points.shape, f32),
        in_specs=[vmem] * 5,
        out_specs=vmem,
        compiler_params=pltpu.CompilerParams(vmem_limit_bytes=VMEM_LIMIT),
        cost_estimate=pl.CostEstimate(flops=2 * 10**9, bytes_accessed=5 * 10**6, transcendentals=0),
        name="point_terms",
    )(slab, points, inv, high, low)


def sum_over(value, axis, size, beside=None):
    if size & (size - 1):
        return lax.psum(value, axis), beside
    steps = [1 << bit for bit in range(size.bit_length() - 1)]
    for place, step in enumerate(steps):
        other = lax.ppermute(value, axis, [(k, k ^ step) for k in range(size)])
        if place == len(steps) - 1 and beside is not None:
            other, beside = lax.optimization_barrier((other, beside))
        value = value + other
    return value, beside


def sum_over_columns(value, mesh, beside):
    size, others = mesh.shape["col"], mesh.shape["row"]
    if size & (size - 1):
        return lax.psum(value, "col"), beside
    bits = [1 << bit for bit in range(size.bit_length() - 1)]
    first = bits.pop(len(bits) // 2)
    even, odd = [first] + bits, bits[:1] + [first] + bits[1:]
    orders = {0: (even, odd), first: (even, odd)}
    if len(bits) > 2:
        orders[first] = [first] + bits[-1:] + bits[:-1], odd
    for place in range(len(even)):
        pairs = [
            (col * others + row, (col ^ orders[col & first][row % 2][place]) * others + row)
            for col in range(size)
            for row in range(others)
        ]
        other = lax.ppermute(value, ("col", "row"), pairs)
        if place == len(even) - 1:
            other, beside = lax.optimization_barrier((other, beside))
        value = value + other
    return value, beside


def solution(mesh):
    def local(slab_embed, slab_probe, point_embed, point_probe, inv_scale):
        inv = inv_scale.reshape(1, -1)
        width = 1024 if point_embed.shape[1] % 1024 == 0 else point_embed.shape[1]
        slab_terms, high, low, slab, points, scale = slab_call(slab_embed, slab_probe, point_embed, point_probe, inv, width)
        point_terms = point_call(slab, points, scale, high, low, width // 2)
        point_grad, _ = sum_over(point_terms, "row", mesh.shape["row"])
        slab_grad, point_grad = sum_over_columns(slab_terms, mesh, point_grad)
        return slab_grad, point_grad

    placed = (P(None, "row"), P(None, "row"), P(None, "col"), P(None, "col"), P())
    return jax.shard_map(
        local, mesh=mesh, in_specs=placed, out_specs=(P(None, "row"), P(None, "col")), check_vma=False
    )
```
